128 devices in a mesh: vocab: 4 (over z_lo, core), fsdp: 32 (over y, z_hi, x).
Axes of the slice: x: 4, y: 4, z: 4 (z_hi: 2, z_lo: 2; z = z_hi * 2 + z_lo), core: 2. Of those that a mesh axis runs over, the one named last changes fastest.
Arguments:
- hidden: bfloat16 [2, 1536, 4096], P(None, 'fsdp'), may hold values from -1000 to 1000
- norm_gain: bfloat16 [4096], replicated, may hold values from 0.5 to 1.5
- labels: int32 [2, 1536], P(None, 'fsdp'), may hold values from 0 to 65535
- head_weight: bfloat16 [4096, 65536], P(None, ('vocab', 'fsdp')), may hold values from -1 to 1
- head_ema: float32 [4096, 65536], P(None, ('vocab', 'fsdp')), may hold values from 1e-09 to 0.001
- gain_ema: float32 [4096], replicated, may hold values from 0.0001 to 0.03
Outputs:
- head_ema_new: float32 [4096, 65536], P(None, ('vocab', 'fsdp'))
- gain_ema_new: float32 [4096], replicated
The draws below stay inside these ranges and needn't reach their ends.
All inputs are finite; a program needn't handle non-finite values.
Results may differ from the reference program's by a relative error of at most 0.00049.
Values may be sent and summed in bfloat16 or wider, within the bound.
No kernel may reach another device: no remote copies, remote signals or barrier semaphores. Data moves between devices by JAX's collectives and lax.ppermute only.
A program may use at most 192 MiB of HBM per device.

```python
import math
import jax
import jax.numpy as jnp
import numpy as np
from jax import lax

D = 4096
V = 65536
MB = 2
TOKENS = 1536


def build_pair(key):
    base_key = jax.random.fold_in(key, 7)
    k_weight, k_common, k_noise, k_rows, k_cols = jax.random.split(base_key, 5)
    weight = jax.random.normal(k_weight, (D, V), jnp.float32) * (3.0 / math.sqrt(D))
    noise = jax.random.normal(k_noise, (MB, TOKENS, D), jnp.float32)
    common = jax.random.normal(k_common, (D,), jnp.float32)
    row_scale = jnp.exp(jax.random.uniform(k_rows, (MB, TOKENS, 1), jnp.float32, 0.0, math.log(10.0)))
    col_scale = jnp.exp(jax.random.uniform(k_cols, (D,), jnp.float32, 0.0, math.log(10.0)))
    states = (noise + common[None, None, :]) * row_scale * col_scale[None, None, :]
    limit = 1.0 + 2600 // D
    states = jnp.clip(states, -1000.0, 1000.0)
    weight = jnp.clip(weight, -limit, limit)
    return (states, weight)


def draw_hidden(key, part):
    states, weight = build_pair(key)
    return states.astype(jnp.bfloat16)


def draw_head_weight(key, part):
    states, weight = build_pair(key)
    return weight.astype(jnp.bfloat16)


def set_ends(values, rng, low, largest):
    extent = values.shape
    index_at = [jax.random.randint(jax.random.fold_in(rng, axis), (), 0, extent[axis]) for axis in range(len(extent))]
    values = values.at[tuple(index_at)].set(low)
    longest = extent.index(max(extent))
    index_at[longest] = (index_at[longest] + 1) % extent[longest]
    return values.at[tuple(index_at)].set(largest)


def block_levels(rng, extent, cuts, smallest, top_value):
    level = 1.0
    for position, shards_of in cuts:
        heights = jax.random.uniform(jax.random.fold_in(jax.random.fold_in(rng, 6), position), (shards_of,), jnp.float32, smallest / len(cuts), top_value / len(cuts))
        level = level * jnp.repeat(jnp.exp(heights), extent[position] // shards_of).reshape((-1,) + (1,) * (len(extent) - 1 - position))
    return level


def rank_table(number_of, skew):
    weights = [(1 << 20) // math.isqrt(rank ** skew) + 1 for rank in range(1, number_of + 1)]
    scale = 1 + sum(weights) // (1 << 30)
    return np.cumsum(np.array([max(1, weight // scale) for weight in weights]))


def ranked_ids(own_key, shape, amount, skew):
    grid = rank_table(amount, skew)
    lot = jax.random.randint(jax.random.fold_in(own_key, 1), shape, 0, int(grid[amount - 1]))
    standing = jnp.searchsorted(jnp.asarray(grid, jnp.int32), lot, side="right")
    return jax.random.permutation(jax.random.fold_in(own_key, 2), amount)[standing].astype(jnp.int32)


def setup_inputs(seed: int = 0) -> dict:
    splits = jax.random.split(jax.random.key(seed), 7)
    return {
        "hidden": draw_hidden(jax.random.fold_in(splits[6], 71), 0),
        "norm_gain": jnp.clip(1.0 + 0.1 * jax.random.normal(splits[1], (D,), jnp.float32), 0.5, 1.5).astype(jnp.bfloat16),
        "labels": set_ends(ranked_ids(splits[2], (MB, TOKENS), V, 2), jax.random.fold_in(splits[2], 3), 0, V - 1).astype(jnp.int32),
        "head_weight": draw_head_weight(jax.random.fold_in(splits[6], 71), 0),
        "head_ema": jnp.clip(jnp.exp(math.log(0.001) - 13.815511 * jax.random.uniform(splits[4], (D, V), jnp.float32) ** block_levels(splits[4], (D, V), ((1, 128),), -0.2, 0.2)), 9.999999717180685e-10, 0.001),
        "gain_ema": jnp.clip(jnp.exp(jax.random.uniform(splits[5], (D,), jnp.float32, math.log(0.0001), math.log(0.03))), 0.0001, 0.03),
    }


BETA = 0.99
EPS = 1e-05

def normalize(hidden, norm_gain):
    wide = hidden.astype(jnp.float32)
    factor = lax.rsqrt(lax.optimization_barrier(jnp.mean(wide * wide, axis=-1, keepdims=True)) + EPS)
    return (wide * factor * norm_gain.astype(jnp.float32)).astype(jnp.bfloat16)

def reference(hidden, norm_gain, labels, head_weight, head_ema, gain_ema):
    scaled = normalize(hidden, norm_gain)
    columns = lax.iota(jnp.int32, V)
    gradient = jnp.zeros((D, V), jnp.float32)
    for batch in range(MB):
        logits = jnp.dot(scaled[batch], head_weight, preferred_element_type=jnp.float32)
        row_top = lax.optimization_barrier(jnp.max(logits, axis=1, keepdims=True))
        shifted = jnp.exp(logits - row_top)
        chances = shifted / lax.optimization_barrier(jnp.sum(shifted, axis=1, keepdims=True))
        hits = (labels[batch][:, None] == columns[None, :]).astype(jnp.float32)
        slope = (chances - hits).astype(jnp.bfloat16)
        gradient = gradient + jnp.dot(scaled[batch].T, slope, preferred_element_type=jnp.float32)
    count = MB * TOKENS
    head_new = BETA * head_ema + (1.0 - BETA) * gradient * gradient / count
    gain_grad = lax.optimization_barrier(jnp.sum(head_weight.astype(jnp.float32) * gradient, axis=1)) / norm_gain.astype(jnp.float32)
    gain_new = BETA * gain_ema + (1.0 - BETA) * gain_grad * gain_grad / count
    return (head_new, gain_new)
```

```python
import functools

import jax
import jax.numpy as jnp
from jax import lax
from jax.experimental import pallas as pl
from jax.experimental.pallas import tpu as pltpu
from jax.sharding import Mesh
from jax.sharding import PartitionSpec as P

AXES = ("zl", "co", "y", "zh", "x")
SIZES = (2, 2, 4, 2, 4)
VOCAB_FSDP = AXES
FSDP = ("y", "zh", "x")

BETA = 0.99
EPS = 1e-05
LANES = 128
ROWS = 16
SETS = (2, 1)
CALLS = (((0, 0),), ((0, 1), (0, 3), (1, 0)), ((0, 2), (1, 1), (1, 3)), ((1, 2),))
TILE = 256
DBLOCK = 512
PART = 256
FORWARD_LIMIT = 16 * 1024 * 1024
VMEM_LIMIT = 60 * 1024 * 1024


def moved(value, target):
    pairs = []
    for source in range(128):
        rest, at = source, []
        for size in reversed(SIZES):
            at.append(rest % size)
            rest //= size
        to = 0
        for size, coordinate in zip(SIZES, target(*reversed(at))):
            to = to * size + coordinate % size
        pairs.append((source, to))
    return lax.ppermute(value, AXES, pairs)


def z_swap(value):
    return moved(value, lambda zl, co, y, zh, x: (1 - zl, co, y, 1 - zh, x))


def core_swap(value):
    return moved(value, lambda zl, co, y, zh, x: (zl, 1 - co, y, zh, x))


def shift(value, step, phase):
    def target(zl, co, y, zh, x):
        if co == phase:
            return (zl, co, y, zh, x + step)
        return (zl, co, y + step, zh, x)

    return moved(value, target)


PAIRINGS = (
    lambda zl, co, y, zh, x: (zl, 1 - co, y, zh, x),
    lambda zl, co, y, zh, x: (1 - zl, co, y, zh, x),
    lambda zl, co, y, zh, x: (1 - zl, co, y, 1 - zh, x),
    lambda zl, co, y, zh, x: (zl, co, y, zh, x ^ 1),
    lambda zl, co, y, zh, x: (zl, co, y, zh, 3 - x),
    lambda zl, co, y, zh, x: (zl, co, y ^ 1, zh, x),
    lambda zl, co, y, zh, x: (zl, co, 3 - y, zh, x),
)


def log_sum(one, two):
    top = jnp.maximum(one, two)
    return top + jnp.log(jnp.exp(one - top) + jnp.exp(two - top))


def slab_of(two, right, far, left):
    groups, _, _, width = two.shape
    return jnp.stack([two, right, far, left], axis=1).reshape(groups * LANES, width)


def forward_kernel(features, sizes, wt_ref, *refs):
    count = len(sizes)
    x_refs, e_ref, stats_ref = refs[:count], refs[count], refs[count + 1]
    picks = lax.broadcasted_iota(jnp.int32, (ROWS, LANES), 0) == lax.broadcasted_iota(jnp.int32, (ROWS, LANES), 1)
    picks = jnp.where(picks, 1.0, 0.0).astype(jnp.bfloat16)
    across = (((1,), (1,)), ((), ()))
    starts = [sum(sizes[:k]) for k in range(count)]
    for at in range(0, sum(sizes), TILE):
        held = [
            (ref, slice(max(at - start, 0), min(at + TILE - start, size)))
            for ref, start, size in zip(x_refs, starts, sizes)
            if start < at + TILE and at < start + size
        ]

        def rows_of(cols):
            parts = [ref[part, cols] for ref, part in held]
            return parts[0] if len(parts) == 1 else jnp.concatenate(parts, axis=0)

        rows = slice(at, at + TILE)
        logits = lax.dot_general(
            wt_ref[...], rows_of(slice(0, features)), across, preferred_element_type=jnp.float32
        )
        top = jnp.max(logits, axis=0, keepdims=True)
        e = jnp.exp(logits - top)
        total = jnp.sum(e, axis=0, keepdims=True)
        e_ref[:, rows] = e
        codes = lax.dot_general(
            picks, rows_of(slice(features, features + LANES)), across, preferred_element_type=jnp.float32
        )
        label = codes[0:1] * 256.0 + codes[1:2]
        for part in range(TILE // LANES):
            row = at // LANES + part
            cols = slice(part * LANES, (part + 1) * LANES)
            stats_ref[0, row : row + 1, :] = top[:, cols]
            stats_ref[1, row : row + 1, :] = total[:, cols]
            stats_ref[2, row : row + 1, :] = label[:, cols]


def forward(wt, buffers, features):
    columns = wt.shape[0]
    sizes = [b.shape[0] for b in buffers]
    tokens = sum(sizes)
    width = buffers[0].shape[1]
    vmem = pl.BlockSpec(memory_space=pltpu.VMEM)
    return pl.pallas_call(
        functools.partial(forward_kernel, features, sizes),
        out_shape=(
            jax.ShapeDtypeStruct((columns, tokens), jnp.float32),
            jax.ShapeDtypeStruct((3, tokens // LANES, LANES), jnp.float32),
        ),
        in_specs=[vmem] * (1 + len(buffers)),
        out_specs=(vmem, vmem),
        compiler_params=pltpu.CompilerParams(vmem_limit_bytes=FORWARD_LIMIT),
        cost_estimate=pl.CostEstimate(
            flops=2 * columns * tokens * features,
            bytes_accessed=2 * tokens * width + 2 * columns * features + 4 * columns * tokens,
            transcendentals=columns * tokens,
        ),
        name="forward",
    )(wt, *buffers)


def aligned(block, lead, zh):
    lane = lax.broadcasted_iota(jnp.int32, block.shape, block.ndim - 1)
    back = pltpu.roll(block, LANES - ROWS, block.ndim - 1)
    ahead = pltpu.roll(block, ROWS, block.ndim - 1)
    swapped = jnp.where((lane // ROWS) % 2 == 0, back, ahead)
    block = jnp.where(zh == 1, swapped, block)
    turned = block
    for k in range(1, 4):
        turned = jnp.where(lead == k, pltpu.roll(block, k * 2 * ROWS, block.ndim - 1), turned)
    return turned


def place_of(place_ref, which):
    core, y, zh, x = (place_ref[k] for k in range(4))
    part = core if which == 0 else 1 - core
    return part, jnp.where(part == 0, y, x), jnp.where(part == 0, x, y), zh


def layout():
    found = {}
    for call, slabs in enumerate(CALLS):
        row = 0
        for which in range(2):
            for part, slab in slabs:
                found[part, which, slab] = (call, row)
                row += SETS[part]
    return found


def first_row(part):
    return sum(8 * groups for groups in SETS[:part])


def canon_kernel(place_ref, *refs):
    stats_refs, out_ref, turned = refs[: len(CALLS)], refs[-2], refs[-1]
    at = layout()
    for part, groups in enumerate(SETS):
        for which in range(2):
            batch, slab0, lane0, zh = place_of(place_ref, which)
            for slab in range(4):
                call, row = at[part, which, slab]
                ref = stats_refs[call]
                sums = ref[0, row : row + groups, :] + jnp.log(ref[1, row : row + groups, :])
                turned[slab * groups : (slab + 1) * groups, :] = sums
            turned[: 4 * groups, :] = aligned(turned[: 4 * groups, :], lane0, zh)
            for slab in range(4):
                to = first_row(part) + (batch * 4 + lax.rem(slab0 + slab, 4)) * groups
                for g in range(groups):
                    row = slab * groups + g
                    out_ref[pl.ds(to + g, 1), :] = turned[row : row + 1, :]


def canonical(place, stats):
    return pl.pallas_call(
        canon_kernel,
        out_shape=jax.ShapeDtypeStruct((first_row(len(SETS)), LANES), jnp.float32),
        in_specs=[pl.BlockSpec(memory_space=pltpu.SMEM)] + [pl.BlockSpec(memory_space=pltpu.VMEM)] * len(stats),
        out_specs=pl.BlockSpec(memory_space=pltpu.VMEM),
        scratch_shapes=[pltpu.VMEM((4 * max(SETS), LANES), jnp.float32)],
        name="canonical",
    )(place, *stats)


def backward_kernel(sizes, widths, count, place_ref, base_ref, *refs):
    calls, buffers = len(CALLS), len(sizes)
    stats_refs, joined_ref, wt_ref, ema_ref = refs[:calls], refs[calls], refs[calls + 1], refs[calls + 2]
    e_refs = refs[calls + 3 : 2 * calls + 3]
    x_refs = refs[2 * calls + 3 : 2 * calls + 3 + buffers]
    new_ref, gain_ref, xs, es, slope, rel, sems, e_sems = refs[2 * calls + 3 + buffers :]
    step, steps = pl.program_id(0), pl.num_programs(0)

    def copies(block, slot):
        at, made = 0, []
        cols = pl.ds(pl.multiple_of(block * DBLOCK, DBLOCK), DBLOCK)
        for k, size in enumerate(sizes):
            made.append(pltpu.make_async_copy(x_refs[k].at[:, cols], xs.at[slot, pl.ds(at, size)], sems.at[slot, k]))
            at += size
        return made

    @pl.when(step == 0)
    def _():
        starts = [sum(widths[:call]) for call in range(calls)]
        e_copies = [
            pltpu.make_async_copy(e_refs[call], es.at[:, pl.ds(starts[call], widths[call])], e_sems.at[call])
            for call in range(calls)
        ]
        for copy in e_copies + copies(0, 0):
            copy.start()
        at = layout()
        columns = es.shape[0]
        ids = lax.broadcasted_iota(jnp.int32, (columns, LANES), 0) + base_ref[0]
        for part, groups in enumerate(SETS):
            for which in range(2):
                batch, slab0, lane0, zh = place_of(place_ref, which)
                for slab in range(4):
                    row = first_row(part) + (batch * 4 + lax.rem(slab0 + slab, 4)) * groups
                    call, to = at[part, which, slab]
                    to += starts[call] // LANES
                    for g in range(groups):
                        rel[to + g : to + g + 1, :] = aligned(joined_ref[pl.ds(row + g, 1), :], lax.rem(4 - lane0, 4), zh)
        for call in range(calls):
            e_copies[call].wait()
            for row in range(widths[call] // LANES):
                k = starts[call] // LANES + row
                cols = slice(k * LANES, (k + 1) * LANES)
                scale = jnp.exp(stats_refs[call][0, row : row + 1, :] - rel[k : k + 1, :])
                hits = ids == stats_refs[call][2, row : row + 1, :].astype(jnp.int32)
                slope[:, cols] = (es[:, cols] * scale - jnp.where(hits, 1.0, 0.0)).astype(jnp.bfloat16)

    @pl.when(step + 1 < steps)
    def _():
        for copy in copies(step + 1, lax.rem(step + 1, 2)):
            copy.start()

    slot = lax.rem(step, 2)
    for copy in copies(step, slot):
        copy.wait()
    for k in range(DBLOCK // PART):
        cols = slice(k * PART, (k + 1) * PART)
        gradient = jnp.dot(slope[...], xs[slot, :, cols], preferred_element_type=jnp.float32)
        gain_ref[:, cols] = jnp.sum(wt_ref[:, cols].astype(jnp.float32) * gradient, axis=0, keepdims=True)
        turned = gradient.T
        new_ref[cols, :] = BETA * ema_ref[cols, :] + (1.0 - BETA) * turned * turned / count


def backward(place, base, stats, joined, es, wt, ema, buffers, count):
    features, columns = ema.shape
    sizes = [b.shape[0] for b in buffers]
    widths = [e.shape[1] for e in es]
    tokens = sum(sizes)
    whole = pl.BlockSpec(memory_space=pltpu.VMEM)
    return pl.pallas_call(
        functools.partial(backward_kernel, sizes, widths, count),
        grid=(features // DBLOCK,),
        out_shape=(
            jax.ShapeDtypeStruct((features, columns), jnp.float32),
            jax.ShapeDtypeStruct((1, features), jnp.float32),
        ),
        in_specs=[
            pl.BlockSpec(memory_space=pltpu.SMEM),
            pl.BlockSpec(memory_space=pltpu.SMEM),
            *[whole] * (len(stats) + 1),
            pl.BlockSpec((columns, DBLOCK), lambda j: (0, j)),
            pl.BlockSpec((DBLOCK, columns), lambda j: (j, 0)),
        ]
        + [pl.BlockSpec(memory_space=pl.ANY)] * (len(es) + len(buffers)),
        out_specs=(
            pl.BlockSpec((DBLOCK, columns), lambda j: (j, 0)),
            pl.BlockSpec((1, DBLOCK), lambda j: (0, j)),
        ),
        scratch_shapes=[
            pltpu.VMEM((2, tokens, DBLOCK), jnp.bfloat16),
            pltpu.VMEM((columns, tokens), jnp.float32),
            pltpu.VMEM((columns, tokens), jnp.bfloat16),
            pltpu.VMEM((tokens // LANES, LANES), jnp.float32),
            pltpu.SemaphoreType.DMA((2, len(buffers))),
            pltpu.SemaphoreType.DMA((len(es),)),
        ],
        compiler_params=pltpu.CompilerParams(
            vmem_limit_bytes=VMEM_LIMIT, dimension_semantics=("arbitrary",)
        ),
        cost_estimate=pl.CostEstimate(
            flops=2 * columns * tokens * features,
            bytes_accessed=2 * tokens * features + 10 * columns * features + 4 * columns * tokens,
            transcendentals=0,
        ),
        name="backward",
    )(place, base, *stats, joined, wt, ema, *es, *buffers)


def on_device(hidden, norm_gain, labels, head_weight, head_ema, gain_ema):
    batches, own_rows, features = hidden.shape
    columns = head_weight.shape[1]
    core = lax.axis_index("co")
    place = jnp.stack([core, lax.axis_index("y"), lax.axis_index("zh"), lax.axis_index("x")]).astype(jnp.int32)
    base = (lax.axis_index(VOCAB_FSDP) * columns).astype(jnp.int32).reshape(1)
    gain_wide = norm_gain.astype(jnp.float32)
    wide = lax.dynamic_index_in_dim(hidden, core, 0, keepdims=False).astype(jnp.float32)
    factor = lax.rsqrt(jnp.mean(wide * wide, axis=-1, keepdims=True) + EPS)
    scaled = (wide * factor * gain_wide).astype(jnp.bfloat16)
    own_labels = lax.dynamic_index_in_dim(labels, core, 0, keepdims=False)[:, None]
    lane = lax.broadcasted_iota(jnp.int32, (own_rows, LANES), 1)
    codes = jnp.where(lane == 0, own_labels // 256, jnp.where(lane == 1, own_labels % 256, 0)).astype(jnp.bfloat16)
    own = jnp.concatenate([scaled, codes], axis=1).reshape(own_rows // ROWS, ROWS, features + LANES)
    count = batches * own_rows * 32
    wt = head_weight.T

    tie = lax.optimization_barrier
    own0, own1 = own[: SETS[0]], own[SETS[0] :]
    z0, z1 = z_swap(own0), z_swap(own1)
    two0 = jnp.stack([own0, z0], axis=1)
    left0, right0 = shift(two0, 1, 0), shift(two0, -1, 0)
    left0, right0, z1, wt = tie((left0, right0, z1, wt))
    two1 = jnp.stack([own1, z1], axis=1)
    far0 = [shift(left0[:, :1], 1, 0), shift(right0[:, 1:], -1, 0)]
    left1, right1 = shift(two1, 1, 0), shift(two1, -1, 0)
    first0 = slab_of(two0, right0, jnp.concatenate(far0, axis=1), left0)
    a_left0, a_right0 = shift(first0, 1, 1), shift(first0, -1, 1)
    far1 = [shift(left1[:, :1], 1, 0), shift(right1[:, 1:], -1, 0)]
    theirs0 = core_swap(first0)
    out0 = forward(wt, [first0, theirs0], features)
    first1 = slab_of(two1, right1, jnp.concatenate(far1, axis=1), left1)
    a_left0, a_right0, first1, out0 = tie((a_left0, a_right0, first1, out0))
    half0, half1 = SETS[0] * LANES // 2, SETS[1] * LANES // 2
    a_far0 = [shift(a_left0[:half0], 1, 1), shift(a_right0[half0:], -1, 1)]
    mine = [[first0], [a_right0, a_left0, first1]]
    theirs = [[theirs0], [core_swap(b) for b in mine[1]]]
    ahead1, theirs[1] = tie((first1, theirs[1]))
    a_left1, a_right1 = shift(ahead1, 1, 1), shift(ahead1, -1, 1)
    out1 = forward(wt, mine[1] + theirs[1], features)
    a_left1, a_right1, out1 = tie((a_left1, a_right1, out1))
    a_far1 = [shift(a_left1[:half1], 1, 1), shift(a_right1[half1:], -1, 1)]
    mine += [a_far0 + [a_right1, a_left1]]
    theirs += [[core_swap(b) for b in mine[2]]]
    out2 = forward(wt, mine[2] + theirs[2], features)
    a_far1[0], a_far1[1], out2 = tie((a_far1[0], a_far1[1], out2))
    theirs += [[core_swap(b) for b in a_far1]]
    mine += [a_far1]
    out3 = forward(wt, a_far1 + theirs[3], features)
    es, stats = zip(out0, out1, out2, out3)
    joined = canonical(place, stats)
    for pairing in PAIRINGS:
        joined = log_sum(joined, moved(joined, pairing))
    buffers = [b for pair in zip(mine, theirs) for side in pair for b in side]
    head_new, partial_sum = backward(place, base, stats, joined, es, wt, head_ema, buffers, count)
    for pairing in PAIRINGS:
        partial_sum = partial_sum + moved(partial_sum, pairing)
    gain_grad = partial_sum[0] / gain_wide
    gain_new = BETA * gain_ema + (1.0 - BETA) * gain_grad * gain_grad / count
    return (head_new, gain_new)


def solution(mesh):
    finer = Mesh(mesh.devices.reshape(SIZES), AXES)
    return jax.shard_map(
        on_device,
        mesh=finer,
        in_specs=(
            P(None, FSDP, None),
            P(),
            P(None, FSDP),
            P(None, VOCAB_FSDP),
            P(None, VOCAB_FSDP),
            P(),
        ),
        out_specs=(P(None, VOCAB_FSDP), P()),
        check_vma=False,
    )
```

```python
import functools

import jax
import jax.numpy as jnp
from jax import lax
from jax.experimental import pallas as pl
from jax.experimental.pallas import tpu as pltpu
from jax.sharding import Mesh
from jax.sharding import PartitionSpec as P

AXES = ("zl", "co", "y", "zh", "x")
SIZES = (2, 2, 4, 2, 4)
VOCAB_FSDP = AXES
FSDP = ("y", "zh", "x")

BETA = 0.99
EPS = 1e-05
LANES = 128
ROWS = 16
SETS = (2, 1)
CALLS = (((0, 0),), ((0, 1), (0, 3), (1, 0)), ((0, 2), (1, 1), (1, 3)), ((1, 2),))
TILE = 256
DBLOCK = 1024
PART = 256
FORWARD_LIMIT = 16 * 1024 * 1024
VMEM_LIMIT = 60 * 1024 * 1024


def moved(value, target):
    pairs = []
    for source in range(128):
        rest, at = source, []
        for size in reversed(SIZES):
            at.append(rest % size)
            rest //= size
        to = 0
        for size, coordinate in zip(SIZES, target(*reversed(at))):
            to = to * size + coordinate % size
        pairs.append((source, to))
    return lax.ppermute(value, AXES, pairs)


def z_swap(value):
    return moved(value, lambda zl, co, y, zh, x: (1 - zl, co, y, 1 - zh, x))


def core_swap(value):
    return moved(value, lambda zl, co, y, zh, x: (zl, 1 - co, y, zh, x))


def shift(value, step, phase):
    def target(zl, co, y, zh, x):
        if co == phase:
            return (zl, co, y, zh, x + step)
        return (zl, co, y + step, zh, x)

    return moved(value, target)


PAIRINGS = (
    lambda zl, co, y, zh, x: (zl, 1 - co, y, zh, x),
    lambda zl, co, y, zh, x: (1 - zl, co, y, zh, x),
    lambda zl, co, y, zh, x: (1 - zl, co, y, 1 - zh, x),
    lambda zl, co, y, zh, x: (zl, co, y, zh, x ^ 1),
    lambda zl, co, y, zh, x: (zl, co, y, zh, 3 - x),
    lambda zl, co, y, zh, x: (zl, co, y ^ 1, zh, x),
    lambda zl, co, y, zh, x: (zl, co, 3 - y, zh, x),
)


def log_sum(one, two):
    top = jnp.maximum(one, two)
    return top + jnp.log(jnp.exp(one - top) + jnp.exp(two - top))


def slab_of(two, right, far, left):
    groups, _, _, width = two.shape
    return jnp.stack([two, right, far, left], axis=1).reshape(groups * LANES, width)


def normalize_kernel(place_ref, labels_ref, hidden_ref, gain_ref, *out_refs):
    core = place_ref[0]
    _, rows, features = hidden_ref.shape
    wide = hidden_ref[core].astype(jnp.float32)
    factor = lax.rsqrt(jnp.mean(wide * wide, axis=-1, keepdims=True) + EPS)
    scaled = (wide * factor * gain_ref[...].astype(jnp.float32)).astype(jnp.bfloat16)
    row = lax.broadcasted_iota(jnp.int32, (rows, LANES), 0)
    lane = lax.broadcasted_iota(jnp.int32, (rows, LANES), 1)
    label = jnp.zeros((rows, LANES), jnp.int32)
    for k in range(rows):
        label = jnp.where(row == k, labels_ref[core, k], label)
    codes = jnp.where(lane == 0, label // 256, jnp.where(lane == 1, label % 256, 0))
    codes = codes.astype(jnp.float32).astype(jnp.bfloat16)
    at = 0
    for out_ref in out_refs:
        held = slice(at, at + out_ref.shape[0])
        out_ref[:, :features] = scaled[held]
        out_ref[:, features:] = codes[held]
        at += out_ref.shape[0]


def normalized(place, labels, hidden, gain):
    _, _, features = hidden.shape
    smem, vmem = pl.BlockSpec(memory_space=pltpu.SMEM), pl.BlockSpec(memory_space=pltpu.VMEM)
    sets = pl.pallas_call(
        normalize_kernel,
        out_shape=[jax.ShapeDtypeStruct((groups * ROWS, features + LANES), jnp.bfloat16) for groups in SETS],
        in_specs=[smem, smem, vmem, vmem],
        out_specs=[vmem] * len(SETS),
        name="normalized",
    )(place, labels, hidden, gain[None])
    return [rows.reshape(groups, ROWS, features + LANES) for rows, groups in zip(sets, SETS)]


def forward_kernel(features, sizes, wt_ref, *refs):
    count = len(sizes)
    x_refs, e_ref, stats_ref = refs[:count], refs[count], refs[count + 1]
    picks = lax.broadcasted_iota(jnp.int32, (ROWS, LANES), 0) == lax.broadcasted_iota(jnp.int32, (ROWS, LANES), 1)
    picks = jnp.where(picks, 1.0, 0.0).astype(jnp.bfloat16)
    across = (((1,), (1,)), ((), ()))
    starts = [sum(sizes[:k]) for k in range(count)]
    for at in range(0, sum(sizes), TILE):
        held = [
            (ref, slice(max(at - start, 0), min(at + TILE - start, size)))
            for ref, start, size in zip(x_refs, starts, sizes)
            if start < at + TILE and at < start + size
        ]

        def rows_of(cols):
            parts = [ref[part, cols] for ref, part in held]
            return parts[0] if len(parts) == 1 else jnp.concatenate(parts, axis=0)

        rows = slice(at, at + TILE)
        logits = lax.dot_general(
            wt_ref[...], rows_of(slice(0, features)), across, preferred_element_type=jnp.float32
        )
        top = jnp.max(logits, axis=0, keepdims=True)
        e = jnp.exp(logits - top)
        total = jnp.sum(e, axis=0, keepdims=True)
        e_ref[:, rows] = e
        codes = lax.dot_general(
            picks, rows_of(slice(features, features + LANES)), across, preferred_element_type=jnp.float32
        )
        label = codes[0:1] * 256.0 + codes[1:2]
        for part in range(TILE // LANES):
            row = at // LANES + part
            cols = slice(part * LANES, (part + 1) * LANES)
            stats_ref[0, row : row + 1, :] = top[:, cols]
            stats_ref[1, row : row + 1, :] = total[:, cols]
            stats_ref[2, row : row + 1, :] = label[:, cols]


def forward(wt, buffers, features):
    columns = wt.shape[0]
    sizes = [b.shape[0] for b in buffers]
    tokens = sum(sizes)
    width = buffers[0].shape[1]
    vmem = pl.BlockSpec(memory_space=pltpu.VMEM)
    return pl.pallas_call(
        functools.partial(forward_kernel, features, sizes),
        out_shape=(
            jax.ShapeDtypeStruct((columns, tokens), jnp.float32),
            jax.ShapeDtypeStruct((3, tokens // LANES, LANES), jnp.float32),
        ),
        in_specs=[vmem] * (1 + len(buffers)),
        out_specs=(vmem, vmem),
        compiler_params=pltpu.CompilerParams(vmem_limit_bytes=FORWARD_LIMIT),
        cost_estimate=pl.CostEstimate(
            flops=2 * columns * tokens * features,
            bytes_accessed=2 * tokens * width + 2 * columns * features + 4 * columns * tokens,
            transcendentals=columns * tokens,
        ),
        name="forward",
    )(wt, *buffers)


def aligned(block, lead, zh):
    lane = lax.broadcasted_iota(jnp.int32, block.shape, block.ndim - 1)
    back = pltpu.roll(block, LANES - ROWS, block.ndim - 1)
    ahead = pltpu.roll(block, ROWS, block.ndim - 1)
    swapped = jnp.where((lane // ROWS) % 2 == 0, back, ahead)
    block = jnp.where(zh == 1, swapped, block)
    turned = block
    for k in range(1, 4):
        turned = jnp.where(lead == k, pltpu.roll(block, k * 2 * ROWS, block.ndim - 1), turned)
    return turned


def place_of(place_ref, which):
    core, y, zh, x = (place_ref[k] for k in range(4))
    part = core if which == 0 else 1 - core
    return part, jnp.where(part == 0, y, x), jnp.where(part == 0, x, y), zh


def layout():
    found = {}
    for call, slabs in enumerate(CALLS):
        row = 0
        for which in range(2):
            for part, slab in slabs:
                found[part, which, slab] = (call, row)
                row += SETS[part]
    return found


def first_row(part):
    return sum(8 * groups for groups in SETS[:part])


def canon_kernel(place_ref, *refs):
    stats_refs, out_ref, turned = refs[: len(CALLS)], refs[-2], refs[-1]
    at = layout()
    for part, groups in enumerate(SETS):
        for which in range(2):
            batch, slab0, lane0, zh = place_of(place_ref, which)
            for slab in range(4):
                call, row = at[part, which, slab]
                ref = stats_refs[call]
                sums = ref[0, row : row + groups, :] + jnp.log(ref[1, row : row + groups, :])
                turned[slab * groups : (slab + 1) * groups, :] = sums
            turned[: 4 * groups, :] = aligned(turned[: 4 * groups, :], lane0, zh)
            for slab in range(4):
                to = first_row(part) + (batch * 4 + lax.rem(slab0 + slab, 4)) * groups
                for g in range(groups):
                    row = slab * groups + g
                    out_ref[pl.ds(to + g, 1), :] = turned[row : row + 1, :]


def canonical(place, stats):
    return pl.pallas_call(
        canon_kernel,
        out_shape=jax.ShapeDtypeStruct((first_row(len(SETS)), LANES), jnp.float32),
        in_specs=[pl.BlockSpec(memory_space=pltpu.SMEM)] + [pl.BlockSpec(memory_space=pltpu.VMEM)] * len(stats),
        out_specs=pl.BlockSpec(memory_space=pltpu.VMEM),
        scratch_shapes=[pltpu.VMEM((4 * max(SETS), LANES), jnp.float32)],
        name="canonical",
    )(place, *stats)


def backward_kernel(sizes, widths, count, place_ref, base_ref, *refs):
    calls, buffers = len(CALLS), len(sizes)
    stats_refs, joined_ref, wt_ref, ema_ref = refs[:calls], refs[calls], refs[calls + 1], refs[calls + 2]
    e_refs = refs[calls + 3 : 2 * calls + 3]
    x_refs = refs[2 * calls + 3 : 2 * calls + 3 + buffers]
    new_ref, gain_ref, xs, es, slope, rel, sems, e_sems = refs[2 * calls + 3 + buffers :]
    step, steps = pl.program_id(0), pl.num_programs(0)

    def copies(block, slot):
        at, made = 0, []
        cols = pl.ds(pl.multiple_of(block * DBLOCK, DBLOCK), DBLOCK)
        for k, size in enumerate(sizes):
            made.append(pltpu.make_async_copy(x_refs[k].at[:, cols], xs.at[slot, pl.ds(at, size)], sems.at[slot, k]))
            at += size
        return made

    @pl.when(step == 0)
    def _():
        starts = [sum(widths[:call]) for call in range(calls)]
        e_copies = [
            pltpu.make_async_copy(e_refs[call], es.at[:, pl.ds(starts[call], widths[call])], e_sems.at[call])
            for call in range(calls)
        ]
        for copy in e_copies + copies(0, 0):
            copy.start()
        at = layout()
        columns = es.shape[0]
        ids = lax.broadcasted_iota(jnp.int32, (columns, LANES), 0) + base_ref[0]
        for part, groups in enumerate(SETS):
            for which in range(2):
                batch, slab0, lane0, zh = place_of(place_ref, which)
                for slab in range(4):
                    row = first_row(part) + (batch * 4 + lax.rem(slab0 + slab, 4)) * groups
                    call, to = at[part, which, slab]
                    to += starts[call] // LANES
                    for g in range(groups):
                        rel[to + g : to + g + 1, :] = aligned(joined_ref[pl.ds(row + g, 1), :], lax.rem(4 - lane0, 4), zh)
        for call in range(calls):
            e_copies[call].wait()
            for row in range(widths[call] // LANES):
                k = starts[call] // LANES + row
                cols = slice(k * LANES, (k + 1) * LANES)
                scale = jnp.exp(stats_refs[call][0, row : row + 1, :] - rel[k : k + 1, :])
                hits = ids == stats_refs[call][2, row : row + 1, :].astype(jnp.int32)
                slope[:, cols] = (es[:, cols] * scale - jnp.where(hits, 1.0, 0.0)).astype(jnp.bfloat16)

    @pl.when(step + 1 < steps)
    def _():
        for copy in copies(step + 1, lax.rem(step + 1, 2)):
            copy.start()

    slot = lax.rem(step, 2)
    for copy in copies(step, slot):
        copy.wait()
    for k in range(DBLOCK // PART):
        cols = slice(k * PART, (k + 1) * PART)
        gradient = jnp.dot(slope[...], xs[slot, :, cols], preferred_element_type=jnp.float32)
        gain_ref[:, cols] = jnp.sum(wt_ref[:, cols].astype(jnp.float32) * gradient, axis=0, keepdims=True)
        turned = gradient.T
        new_ref[cols, :] = BETA * ema_ref[cols, :] + (1.0 - BETA) * turned * turned / count


def backward(place, base, stats, joined, es, wt, ema, buffers, count):
    features, columns = ema.shape
    sizes = [b.shape[0] for b in buffers]
    widths = [e.shape[1] for e in es]
    tokens = sum(sizes)
    whole = pl.BlockSpec(memory_space=pltpu.VMEM)
    return pl.pallas_call(
        functools.partial(backward_kernel, sizes, widths, count),
        grid=(features // DBLOCK,),
        out_shape=(
            jax.ShapeDtypeStruct((features, columns), jnp.float32),
            jax.ShapeDtypeStruct((1, features), jnp.float32),
        ),
        in_specs=[
            pl.BlockSpec(memory_space=pltpu.SMEM),
            pl.BlockSpec(memory_space=pltpu.SMEM),
            *[whole] * (len(stats) + 1),
            pl.BlockSpec((columns, DBLOCK), lambda j: (0, j)),
            pl.BlockSpec((DBLOCK, columns), lambda j: (j, 0)),
        ]
        + [pl.BlockSpec(memory_space=pl.ANY)] * (len(es) + len(buffers)),
        out_specs=(
            pl.BlockSpec((DBLOCK, columns), lambda j: (j, 0)),
            pl.BlockSpec((1, DBLOCK), lambda j: (0, j)),
        ),
        scratch_shapes=[
            pltpu.VMEM((2, tokens, DBLOCK), jnp.bfloat16),
            pltpu.VMEM((columns, tokens), jnp.float32),
            pltpu.VMEM((columns, tokens), jnp.bfloat16),
            pltpu.VMEM((tokens // LANES, LANES), jnp.float32),
            pltpu.SemaphoreType.DMA((2, len(buffers))),
            pltpu.SemaphoreType.DMA((len(es),)),
        ],
        compiler_params=pltpu.CompilerParams(
            vmem_limit_bytes=VMEM_LIMIT, dimension_semantics=("arbitrary",)
        ),
        cost_estimate=pl.CostEstimate(
            flops=2 * columns * tokens * features,
            bytes_accessed=2 * tokens * features + 10 * columns * features + 4 * columns * tokens,
            transcendentals=0,
        ),
        name="backward",
    )(place, base, *stats, joined, wt, ema, *es, *buffers)


def on_device(hidden, norm_gain, labels, head_weight, head_ema, gain_ema):
    batches, own_rows, features = hidden.shape
    columns = head_weight.shape[1]
    core = lax.axis_index("co")
    place = jnp.stack([core, lax.axis_index("y"), lax.axis_index("zh"), lax.axis_index("x")]).astype(jnp.int32)
    base = (lax.axis_index(VOCAB_FSDP) * columns).astype(jnp.int32).reshape(1)
    gain_wide = norm_gain.astype(jnp.float32)
    own0, own1 = normalized(place, labels, hidden, norm_gain)
    count = batches * own_rows * 32
    wt = head_weight.T

    tie = lax.optimization_barrier
    z0, z1 = z_swap(own0), z_swap(own1)
    z0, wt = tie((z0, wt))
    two0 = jnp.stack([own0, z0], axis=1)
    left0, right0 = shift(two0, 1, 0), shift(two0, -1, 0)
    left0, right0, z1 = tie((left0, right0, z1))
    two1 = jnp.stack([own1, z1], axis=1)
    far0 = [shift(left0[:, :1], 1, 0), shift(right0[:, 1:], -1, 0)]
    left1, right1 = shift(two1, 1, 0), shift(two1, -1, 0)
    first0 = slab_of(two0, right0, jnp.concatenate(far0, axis=1), left0)
    a_left0, a_right0 = shift(first0, 1, 1), shift(first0, -1, 1)
    far1 = [shift(left1[:, :1], 1, 0), shift(right1[:, 1:], -1, 0)]
    theirs0 = core_swap(first0)
    out0 = forward(wt, [first0, theirs0], features)
    first1 = slab_of(two1, right1, jnp.concatenate(far1, axis=1), left1)
    a_left0, a_right0, first1, out0 = tie((a_left0, a_right0, first1, out0))
    half0, half1 = SETS[0] * LANES // 2, SETS[1] * LANES // 2
    a_far0 = [shift(a_left0[:half0], 1, 1), shift(a_right0[half0:], -1, 1)]
    mine = [[first0], [a_right0, a_left0, first1]]
    theirs = [[theirs0], [core_swap(b) for b in mine[1]]]
    ahead1, theirs[1] = tie((first1, theirs[1]))
    a_left1, a_right1 = shift(ahead1, 1, 1), shift(ahead1, -1, 1)
    out1 = forward(wt, mine[1] + theirs[1], features)
    a_left1, a_right1, out1 = tie((a_left1, a_right1, out1))
    a_far1 = [shift(a_left1[:half1], 1, 1), shift(a_right1[half1:], -1, 1)]
    mine += [a_far0 + [a_right1, a_left1]]
    theirs += [[core_swap(b) for b in mine[2]]]
    out2 = forward(wt, mine[2] + theirs[2], features)
    a_far1[0], a_far1[1], out2 = tie((a_far1[0], a_far1[1], out2))
    theirs += [[core_swap(b) for b in a_far1]]
    mine += [a_far1]
    out3 = forward(wt, a_far1 + theirs[3], features)
    es, stats = zip(out0, out1, out2, out3)
    joined = canonical(place, stats)
    for pairing in PAIRINGS:
        joined = log_sum(joined, moved(joined, pairing))
    buffers = [b for pair in zip(mine, theirs) for side in pair for b in side]
    head_new, partial_sum = backward(place, base, stats, joined, es, wt, head_ema, buffers, count)
    for pairing in PAIRINGS:
        partial_sum = partial_sum + moved(partial_sum, pairing)
    gain_grad = partial_sum[0] / gain_wide
    gain_new = BETA * gain_ema + (1.0 - BETA) * gain_grad * gain_grad / count
    return (head_new, gain_new)


def solution(mesh):
    finer = Mesh(mesh.devices.reshape(SIZES), AXES)
    return jax.shard_map(
        on_device,
        mesh=finer,
        in_specs=(
            P(None, FSDP, None),
            P(),
            P(None, FSDP),
            P(None, VOCAB_FSDP),
            P(None, VOCAB_FSDP),
            P(),
        ),
        out_specs=(P(None, VOCAB_FSDP), P()),
        check_vma=False,
    )
```

```python
import functools

import jax
import jax.numpy as jnp
from jax import lax
from jax.experimental import pallas as pl
from jax.experimental.pallas import tpu as pltpu
from jax.sharding import Mesh
from jax.sharding import PartitionSpec as P

AXES = ("zl", "co", "y", "zh", "x")
SIZES = (2, 2, 4, 2, 4)
VOCAB_FSDP = AXES
FSDP = ("y", "zh", "x")

BETA = 0.99
EPS = 1e-05
LANES = 128
ROWS = 16
SETS = (2, 1)
CALLS = (((0, 0),), ((0, 1), (0, 3), (1, 0)), ((0, 2), (1, 1), (1, 3)), ((1, 2),))
TILE = 256
DBLOCK = 1024
PART = 256
FORWARD_LIMIT = 16 * 1024 * 1024
VMEM_LIMIT = 60 * 1024 * 1024


def moved(value, target):
    pairs = []
    for source in range(128):
        rest, at = source, []
        for size in reversed(SIZES):
            at.append(rest % size)
            rest //= size
        to = 0
        for size, coordinate in zip(SIZES, target(*reversed(at))):
            to = to * size + coordinate % size
        pairs.append((source, to))
    return lax.ppermute(value, AXES, pairs)


def z_swap(value):
    return moved(value, lambda zl, co, y, zh, x: (1 - zl, co, y, 1 - zh, x))


def core_swap(value):
    return moved(value, lambda zl, co, y, zh, x: (zl, 1 - co, y, zh, x))


def shift(value, step, phase):
    def target(zl, co, y, zh, x):
        if co == phase:
            return (zl, co, y, zh, x + step)
        return (zl, co, y + step, zh, x)

    return moved(value, target)


PAIRINGS = (
    lambda zl, co, y, zh, x: (zl, 1 - co, y, zh, x),
    lambda zl, co, y, zh, x: (1 - zl, co, y, zh, x),
    lambda zl, co, y, zh, x: (1 - zl, co, y, 1 - zh, x),
    lambda zl, co, y, zh, x: (zl, co, y, zh, x ^ 1),
    lambda zl, co, y, zh, x: (zl, co, y, zh, 3 - x),
    lambda zl, co, y, zh, x: (zl, co, y ^ 1, zh, x),
    lambda zl, co, y, zh, x: (zl, co, 3 - y, zh, x),
)


def log_sum(one, two):
    top = jnp.maximum(one, two)
    return top + jnp.log(jnp.exp(one - top) + jnp.exp(two - top))


def slab_of(two, right, far, left):
    groups, _, _, width = two.shape
    return jnp.stack([two, right, far, left], axis=1).reshape(groups * LANES, width)


def normalize_kernel(labels_ref, hidden_ref, gain_ref, *out_refs):
    core = lax.axis_index("co")
    _, rows, features = hidden_ref.shape
    wide = hidden_ref[core].astype(jnp.float32)
    factor = lax.rsqrt(jnp.mean(wide * wide, axis=-1, keepdims=True) + EPS)
    scaled = (wide * factor * gain_ref[...].astype(jnp.float32)[None]).astype(jnp.bfloat16)
    row = lax.broadcasted_iota(jnp.int32, (rows, LANES), 0)
    lane = lax.broadcasted_iota(jnp.int32, (rows, LANES), 1)
    label = jnp.zeros((rows, LANES), jnp.int32)
    for k in range(rows):
        label = jnp.where(row == k, labels_ref[core, k], label)
    codes = jnp.where(lane == 0, label // 256, jnp.where(lane == 1, label % 256, 0))
    codes = codes.astype(jnp.float32).astype(jnp.bfloat16)
    at = 0
    for out_ref in out_refs:
        held = slice(at, at + out_ref.shape[0])
        out_ref[:, :features] = scaled[held]
        out_ref[:, features:] = codes[held]
        at += out_ref.shape[0]


def normalized(labels, hidden, gain):
    _, _, features = hidden.shape
    smem, vmem = pl.BlockSpec(memory_space=pltpu.SMEM), pl.BlockSpec(memory_space=pltpu.VMEM)
    sets = pl.pallas_call(
        normalize_kernel,
        out_shape=[jax.ShapeDtypeStruct((groups * ROWS, features + LANES), jnp.bfloat16) for groups in SETS],
        in_specs=[smem, vmem, vmem],
        out_specs=[vmem] * len(SETS),
        name="normalized",
    )(labels, hidden, gain)
    return [rows.reshape(groups, ROWS, features + LANES) for rows, groups in zip(sets, SETS)]


def forward_kernel(features, sizes, wt_ref, *refs):
    count = len(sizes)
    x_refs, e_ref, stats_ref = refs[:count], refs[count], refs[count + 1]
    picks = lax.broadcasted_iota(jnp.int32, (ROWS, LANES), 0) == lax.broadcasted_iota(jnp.int32, (ROWS, LANES), 1)
    picks = jnp.where(picks, 1.0, 0.0).astype(jnp.bfloat16)
    across = (((1,), (1,)), ((), ()))
    starts = [sum(sizes[:k]) for k in range(count)]
    for at in range(0, sum(sizes), TILE):
        held = [
            (ref, slice(max(at - start, 0), min(at + TILE - start, size)))
            for ref, start, size in zip(x_refs, starts, sizes)
            if start < at + TILE and at < start + size
        ]

        def rows_of(cols):
            parts = [ref[part, cols] for ref, part in held]
            return parts[0] if len(parts) == 1 else jnp.concatenate(parts, axis=0)

        rows = slice(at, at + TILE)
        logits = lax.dot_general(
            wt_ref[...], rows_of(slice(0, features)), across, preferred_element_type=jnp.float32
        )
        top = jnp.max(logits, axis=0, keepdims=True)
        e = jnp.exp(logits - top)
        total = jnp.sum(e, axis=0, keepdims=True)
        e_ref[:, rows] = e
        codes = lax.dot_general(
            picks, rows_of(slice(features, features + LANES)), across, preferred_element_type=jnp.float32
        )
        label = codes[0:1] * 256.0 + codes[1:2]
        for part in range(TILE // LANES):
            row = at // LANES + part
            cols = slice(part * LANES, (part + 1) * LANES)
            stats_ref[0, row : row + 1, :] = top[:, cols]
            stats_ref[1, row : row + 1, :] = total[:, cols]
            stats_ref[2, row : row + 1, :] = label[:, cols]


def forward(wt, buffers, features):
    columns = wt.shape[0]
    sizes = [b.shape[0] for b in buffers]
    tokens = sum(sizes)
    width = buffers[0].shape[1]
    vmem = pl.BlockSpec(memory_space=pltpu.VMEM)
    return pl.pallas_call(
        functools.partial(forward_kernel, features, sizes),
        out_shape=(
            jax.ShapeDtypeStruct((columns, tokens), jnp.float32),
            jax.ShapeDtypeStruct((3, tokens // LANES, LANES), jnp.float32),
        ),
        in_specs=[vmem] * (1 + len(buffers)),
        out_specs=(vmem, vmem),
        compiler_params=pltpu.CompilerParams(vmem_limit_bytes=FORWARD_LIMIT),
        cost_estimate=pl.CostEstimate(
            flops=2 * columns * tokens * features,
            bytes_accessed=2 * tokens * width + 2 * columns * features + 4 * columns * tokens,
            transcendentals=columns * tokens,
        ),
        name="forward",
    )(wt, *buffers)


def aligned(block, lead, zh):
    lane = lax.broadcasted_iota(jnp.int32, block.shape, block.ndim - 1)
    back = pltpu.roll(block, LANES - ROWS, block.ndim - 1)
    ahead = pltpu.roll(block, ROWS, block.ndim - 1)
    swapped = jnp.where((lane // ROWS) % 2 == 0, back, ahead)
    block = jnp.where(zh == 1, swapped, block)
    turned = block
    for k in range(1, 4):
        turned = jnp.where(lead == k, pltpu.roll(block, k * 2 * ROWS, block.ndim - 1), turned)
    return turned


def place_of(place_ref, which):
    core, y, zh, x = (place_ref[k] for k in range(4))
    part = core if which == 0 else 1 - core
    return part, jnp.where(part == 0, y, x), jnp.where(part == 0, x, y), zh


def layout():
    found = {}
    for call, slabs in enumerate(CALLS):
        row = 0
        for which in range(2):
            for part, slab in slabs:
                found[part, which, slab] = (call, row)
                row += SETS[part]
    return found


def first_row(part):
    return sum(8 * groups for groups in SETS[:part])


def canon_kernel(place_ref, *refs):
    stats_refs, out_ref, turned = refs[: len(CALLS)], refs[-2], refs[-1]
    at = layout()
    for part, groups in enumerate(SETS):
        for which in range(2):
            batch, slab0, lane0, zh = place_of(place_ref, which)
            for slab in range(4):
                call, row = at[part, which, slab]
                ref = stats_refs[call]
                sums = ref[0, row : row + groups, :] + jnp.log(ref[1, row : row + groups, :])
                turned[slab * groups : (slab + 1) * groups, :] = sums
            turned[: 4 * groups, :] = aligned(turned[: 4 * groups, :], lane0, zh)
            for slab in range(4):
                to = first_row(part) + (batch * 4 + lax.rem(slab0 + slab, 4)) * groups
                for g in range(groups):
                    row = slab * groups + g
                    out_ref[pl.ds(to + g, 1), :] = turned[row : row + 1, :]


def canonical(place, stats):
    return pl.pallas_call(
        canon_kernel,
        out_shape=jax.ShapeDtypeStruct((first_row(len(SETS)), LANES), jnp.float32),
        in_specs=[pl.BlockSpec(memory_space=pltpu.SMEM)] + [pl.BlockSpec(memory_space=pltpu.VMEM)] * len(stats),
        out_specs=pl.BlockSpec(memory_space=pltpu.VMEM),
        scratch_shapes=[pltpu.VMEM((4 * max(SETS), LANES), jnp.float32)],
        name="canonical",
    )(place, *stats)


def backward_kernel(sizes, widths, count, place_ref, base_ref, *refs):
    calls, buffers = len(CALLS), len(sizes)
    stats_refs, joined_ref, wt_ref, ema_ref = refs[:calls], refs[calls], refs[calls + 1], refs[calls + 2]
    e_refs = refs[calls + 3 : 2 * calls + 3]
    x_refs = refs[2 * calls + 3 : 2 * calls + 3 + buffers]
    new_ref, gain_ref, xs, es, slope, rel, sems, e_sems = refs[2 * calls + 3 + buffers :]
    step, steps = pl.program_id(0), pl.num_programs(0)

    def copies(block, slot):
        at, made = 0, []
        cols = pl.ds(pl.multiple_of(block * DBLOCK, DBLOCK), DBLOCK)
        for k, size in enumerate(sizes):
            made.append(pltpu.make_async_copy(x_refs[k].at[:, cols], xs.at[slot, pl.ds(at, size)], sems.at[slot, k]))
            at += size
        return made

    @pl.when(step == 0)
    def _():
        starts = [sum(widths[:call]) for call in range(calls)]
        e_copies = [
            pltpu.make_async_copy(e_refs[call], es.at[:, pl.ds(starts[call], widths[call])], e_sems.at[call])
            for call in range(calls)
        ]
        for copy in e_copies + copies(0, 0):
            copy.start()
        at = layout()
        columns = es.shape[0]
        ids = lax.broadcasted_iota(jnp.int32, (columns, LANES), 0) + base_ref[0]
        for part, groups in enumerate(SETS):
            for which in range(2):
                batch, slab0, lane0, zh = place_of(place_ref, which)
                for slab in range(4):
                    row = first_row(part) + (batch * 4 + lax.rem(slab0 + slab, 4)) * groups
                    call, to = at[part, which, slab]
                    to += starts[call] // LANES
                    for g in range(groups):
                        rel[to + g : to + g + 1, :] = aligned(joined_ref[pl.ds(row + g, 1), :], lax.rem(4 - lane0, 4), zh)
        for call in range(calls):
            e_copies[call].wait()
            for row in range(widths[call] // LANES):
                k = starts[call] // LANES + row
                cols = slice(k * LANES, (k + 1) * LANES)
                scale = jnp.exp(stats_refs[call][0, row : row + 1, :] - rel[k : k + 1, :])
                hits = ids == stats_refs[call][2, row : row + 1, :].astype(jnp.int32)
                slope[:, cols] = (es[:, cols] * scale - jnp.where(hits, 1.0, 0.0)).astype(jnp.bfloat16)

    @pl.when(step + 1 < steps)
    def _():
        for copy in copies(step + 1, lax.rem(step + 1, 2)):
            copy.start()

    slot = lax.rem(step, 2)
    for copy in copies(step, slot):
        copy.wait()
    for k in range(DBLOCK // PART):
        cols = slice(k * PART, (k + 1) * PART)
        gradient = jnp.dot(slope[...], xs[slot, :, cols], preferred_element_type=jnp.float32)
        gain_ref[:, cols] = jnp.sum(wt_ref[:, cols].astype(jnp.float32) * gradient, axis=0, keepdims=True)
        turned = gradient.T
        new_ref[cols, :] = BETA * ema_ref[cols, :] + (1.0 - BETA) * turned * turned / count


def backward(place, base, stats, joined, es, wt, ema, buffers, count):
    features, columns = ema.shape
    sizes = [b.shape[0] for b in buffers]
    widths = [e.shape[1] for e in es]
    tokens = sum(sizes)
    whole = pl.BlockSpec(memory_space=pltpu.VMEM)
    return pl.pallas_call(
        functools.partial(backward_kernel, sizes, widths, count),
        grid=(features // DBLOCK,),
        out_shape=(
            jax.ShapeDtypeStruct((features, columns), jnp.float32),
            jax.ShapeDtypeStruct((1, features), jnp.float32),
        ),
        in_specs=[
            pl.BlockSpec(memory_space=pltpu.SMEM),
            pl.BlockSpec(memory_space=pltpu.SMEM),
            *[whole] * (len(stats) + 1),
            pl.BlockSpec((columns, DBLOCK), lambda j: (0, j)),
            pl.BlockSpec((DBLOCK, columns), lambda j: (j, 0)),
        ]
        + [pl.BlockSpec(memory_space=pl.ANY)] * (len(es) + len(buffers)),
        out_specs=(
            pl.BlockSpec((DBLOCK, columns), lambda j: (j, 0)),
            pl.BlockSpec((1, DBLOCK), lambda j: (0, j)),
        ),
        scratch_shapes=[
            pltpu.VMEM((2, tokens, DBLOCK), jnp.bfloat16),
            pltpu.VMEM((columns, tokens), jnp.float32),
            pltpu.VMEM((columns, tokens), jnp.bfloat16),
            pltpu.VMEM((tokens // LANES, LANES), jnp.float32),
            pltpu.SemaphoreType.DMA((2, len(buffers))),
            pltpu.SemaphoreType.DMA((len(es),)),
        ],
        compiler_params=pltpu.CompilerParams(
            vmem_limit_bytes=VMEM_LIMIT, dimension_semantics=("arbitrary",)
        ),
        cost_estimate=pl.CostEstimate(
            flops=2 * columns * tokens * features,
            bytes_accessed=2 * tokens * features + 10 * columns * features + 4 * columns * tokens,
            transcendentals=0,
        ),
        name="backward",
    )(place, base, *stats, joined, wt, ema, *es, *buffers)


def on_device(hidden, norm_gain, labels, head_weight, head_ema, gain_ema):
    batches, own_rows, features = hidden.shape
    columns = head_weight.shape[1]
    core = lax.axis_index("co")
    place = jnp.stack([core, lax.axis_index("y"), lax.axis_index("zh"), lax.axis_index("x")]).astype(jnp.int32)
    base = (lax.axis_index(VOCAB_FSDP) * columns).astype(jnp.int32).reshape(1)
    gain_wide = norm_gain.astype(jnp.float32)
    own0, own1 = normalized(labels, hidden, norm_gain)
    count = batches * own_rows * 32
    wt = head_weight.T

    tie = lax.optimization_barrier
    z0, z1 = z_swap(own0), z_swap(own1)
    z0, wt = tie((z0, wt))
    two0 = jnp.stack([own0, z0], axis=1)
    left0, right0 = shift(two0, 1, 0), shift(two0, -1, 0)
    left0, right0, z1 = tie((left0, right0, z1))
    two1 = jnp.stack([own1, z1], axis=1)
    far0 = [shift(left0[:, :1], 1, 0), shift(right0[:, 1:], -1, 0)]
    left1, right1 = shift(two1, 1, 0), shift(two1, -1, 0)
    first0 = slab_of(two0, right0, jnp.concatenate(far0, axis=1), left0)
    a_left0, a_right0 = shift(first0, 1, 1), shift(first0, -1, 1)
    far1 = [shift(left1[:, :1], 1, 0), shift(right1[:, 1:], -1, 0)]
    theirs0 = core_swap(first0)
    out0 = forward(wt, [first0, theirs0], features)
    first1 = slab_of(two1, right1, jnp.concatenate(far1, axis=1), left1)
    a_left0, a_right0, first1, out0 = tie((a_left0, a_right0, first1, out0))
    half0, half1 = SETS[0] * LANES // 2, SETS[1] * LANES // 2
    a_far0 = [shift(a_left0[:half0], 1, 1), shift(a_right0[half0:], -1, 1)]
    mine = [[first0], [a_right0, a_left0, first1]]
    theirs = [[theirs0], [core_swap(b) for b in mine[1]]]
    ahead1, theirs[1] = tie((first1, theirs[1]))
    a_left1, a_right1 = shift(ahead1, 1, 1), shift(ahead1, -1, 1)
    out1 = forward(wt, mine[1] + theirs[1], features)
    a_left1, a_right1, out1 = tie((a_left1, a_right1, out1))
    a_far1 = [shift(a_left1[:half1], 1, 1), shift(a_right1[half1:], -1, 1)]
    mine += [a_far0 + [a_right1, a_left1]]
    theirs += [[core_swap(b) for b in mine[2]]]
    out2 = forward(wt, mine[2] + theirs[2], features)
    a_far1[0], a_far1[1], out2 = tie((a_far1[0], a_far1[1], out2))
    theirs += [[core_swap(b) for b in a_far1]]
    mine += [a_far1]
    out3 = forward(wt, a_far1 + theirs[3], features)
    es, stats = zip(out0, out1, out2, out3)
    joined = canonical(place, stats)
    for pairing in PAIRINGS:
        joined = log_sum(joined, moved(joined, pairing))
    buffers = [b for pair in zip(mine, theirs) for side in pair for b in side]
    head_new, partial_sum = backward(place, base, stats, joined, es, wt, head_ema, buffers, count)
    for pairing in PAIRINGS:
        partial_sum = partial_sum + moved(partial_sum, pairing)
    gain_grad = partial_sum[0] / gain_wide
    gain_new = BETA * gain_ema + (1.0 - BETA) * gain_grad * gain_grad / count
    return (head_new, gain_new)


def solution(mesh):
    finer = Mesh(mesh.devices.reshape(SIZES), AXES)
    return jax.shard_map(
        on_device,
        mesh=finer,
        in_specs=(
            P(None, FSDP, None),
            P(),
            P(None, FSDP),
            P(None, VOCAB_FSDP),
            P(None, VOCAB_FSDP),
            P(),
        ),
        out_specs=(P(None, VOCAB_FSDP), P()),
        check_vma=False,
    )
```
